128 devices in a mesh: dp: 16 (over y, x), expert: 8 (over z, core).
Axes of the slice: x: 4, y: 4, z: 4, core: 2. Of those that a mesh axis runs over, the one named last changes fastest.
Arguments:
- moe_in: bfloat16 [2048, 4096], P(('dp', 'expert')), may hold values from -6 to 6
- route_expert: int32 [2048, 8], P(('dp', 'expert')), may hold values from 0 to 63, all different within a row; in each aligned block of 16 rows (0 to 15, 16 to 31, ...) at most 2 rows name the same one
- route_weight: float32 [2048, 8], P(('dp', 'expert')), may hold values from 0.05 to 1
- expert_gate_up: bfloat16 [128, 4096, 1536], P(('dp', 'expert')), may hold values from -0.09375 to 0.09375
- expert_down: bfloat16 [128, 768, 4096], P(('dp', 'expert')), may hold values from -0.15625 to 0.15625
- kv_cache: bfloat16 [256, 512, 1024], P(('dp', 'expert')), may hold values from -30 to 30
- decode_query: bfloat16 [256, 8192], P(('dp', 'expert')), may hold values from -30 to 30
- new_kv: bfloat16 [256, 1024], P(('dp', 'expert')), may hold values from -6 to 6
- kv_length: int32 [256], P(('dp', 'expert')), may hold values from 1 to 512, 65536 in all
- decode_group: int32 [256, 1], P(('dp', 'expert')), may hold values from 0 to 15; in each aligned block of 16 rows (0 to 15, 16 to 31, ...) at most 2 rows name the same one
Outputs:
- moe_out: bfloat16 [2048, 4096], P(('dp', 'expert'))
- decode_cache: bfloat16 [512, 512, 1024], P(('dp', 'expert'))
- decode_out: bfloat16 [256, 8192], P('dp', 'expert')
The draws below stay inside these ranges and needn't reach their ends.
Inputs may be any that keep to these rules, and one draw needn't show every extreme that they name: `route_expert`: each token names 8 different experts; at most 2 of the tokens of one device name the same expert, a bound that some block reaches of them. `decode_group`: at most 2 of the prompts of one index of dp name the same group, a bound that some block reaches of them.
All inputs are finite; a program needn't handle non-finite values. No bound on the sum of `kv_length` on one device may be relied on, other than what follows from the above.
Results may differ from the reference program's by a relative error of at most 0.0058.
Values may be sent and summed in bfloat16 or wider, within the bound.
No kernel may reach another device: no remote copies, remote signals or barrier semaphores. Data moves between devices by JAX's collectives and lax.ppermute only.
A program may use at most 128 MiB of HBM per device.

```python
import math
import jax
import jax.numpy as jnp
import numpy as np
from jax import lax

D = 4096
FFE = 1536
TOPK = 8
H = 64
KVH = 4
HD = 128
TOK_DEV = 16
P_DEV = 16
L = 512
BLK = 64
EXPERTS = 64
CAP = 2
TOKENS = 2048
MOSTP = 2
PROMPTS = 256
SLOTS = 32
N_DP = 16
N_EXPERT = 8


def draw_kv_cache(key, part):
    key = jax.random.fold_in(key, 7)
    values = jnp.clip(jax.random.normal(key, (PROMPTS, L, 2 * KVH * HD), jnp.float32), -6.0, 6.0)
    return values.astype(jnp.bfloat16)


def draw_decode_query(key, part):
    key = jax.random.fold_in(key, 5)
    noise_key = jax.random.fold_in(key, 0)
    values = jnp.clip(jax.random.normal(noise_key, (PROMPTS, KVH, H // KVH, HD), jnp.float32), -6.0, 6.0)
    return values.reshape(PROMPTS, H * HD).astype(jnp.bfloat16)


def shard_levels(key, shape, shards, least, largest):
    def one(axis_at, parts):
        heights = jax.random.uniform(jax.random.fold_in(jax.random.fold_in(key, 6), axis_at), (parts,), jnp.float32, least / len(shards), largest / len(shards))
        return jnp.repeat(jnp.exp(heights), shape[axis_at] // parts).reshape((-1,) + (1,) * (len(shape) - axis_at - 1))

    level = one(*shards[0])
    for cut in shards[1:]:
        level = level * one(*cut)
    return level


def split_up(amount, total, reach, lean):
    loads = [(1 << 20) // math.isqrt(standing ** lean) + 1 for standing in range(2, amount + 1)]
    surplus, holding = total - reach - (amount - 1), [1] * (amount - 1)
    while surplus > 0:
        free = [i for i in range(amount - 1) if holding[i] < reach]
        whole, left = sum([loads[i] for i in free]), surplus
        for i in free:
            extra = min(reach - holding[i], max(1, left * loads[i] // whole), surplus)
            holding[i] = holding[i] + extra
            surplus = surplus - extra
    return np.array([reach] + holding)


def uneven(own_key, amount, total, most, slope):
    if amount == 2:
        one = jax.random.randint(own_key, (), max(1, total - most), min(most, total - 1) + 1)
        return jnp.stack([one, total - one])
    tallies = jnp.asarray(split_up(amount, total, most, slope), jnp.int32)
    pairs = (amount - 1) // 2
    source_of, receiver = tallies[1:1 + 2 * pairs:2], tallies[2:2 + 2 * pairs:2]
    slack = jnp.minimum(source_of - 1, most - receiver)
    passed = jax.random.randint(jax.random.fold_in(own_key, 1), (pairs,), 0, 1 << 20) % (slack + 1)
    tallies = tallies.at[1:1 + 2 * pairs:2].set(source_of - passed).at[2:2 + 2 * pairs:2].set(receiver + passed)
    return tallies[jax.random.permutation(jax.random.fold_in(own_key, 2), amount)]


def routed_block(own_key, own, number, rows, count, top, most, skew):
    ranking = jax.random.permutation(own_key, count)
    heavy_load, ordinary = portions_of(count, rows * top, most, skew, True), portions_of(count, rows * top, most, skew, False)
    places = jnp.arange(count)

    def named(tallies, turn):
        used = int((tallies > 0).sum())
        fixed = max(1, used // 4)
        passed = fixed + (places - fixed + turn * (used - fixed)) % max(1, count - fixed)
        return jnp.zeros((count,), jnp.int32).at[ranking[jnp.where(places < fixed, places, passed)]].set(jnp.asarray(tallies, jnp.int32))

    tallies = jnp.where(number % 4 == 0, named(heavy_load, number // 4), named(ordinary, number - number // 4 - 1))
    mixed = jax.random.permutation(jax.random.fold_in(own, 3), count)
    source_of, receiver = mixed[0:count // 2 * 2:2], mixed[1:count // 2 * 2:2]
    margin = jnp.minimum(tallies[source_of] - 1, most - tallies[receiver]) // 2
    margin = jnp.where((source_of == ranking[0]) | (receiver == ranking[0]) | (tallies[receiver] == 0), 0, jnp.maximum(margin, 0))
    passed = jax.random.randint(jax.random.fold_in(own, 4), (count // 2,), 0, 1 << 20) % (margin + 1)
    tallies = tallies.at[source_of].add(-passed).at[receiver].add(passed)
    members = jnp.searchsorted(jnp.cumsum(tallies), jnp.arange(rows * top), side="right").astype(jnp.int32)
    grid = members.reshape(top, rows).T
    grid = grid[jax.random.permutation(jax.random.fold_in(own, 1), rows)]
    turn = jax.random.randint(jax.random.fold_in(own, 2), (rows, 1), 0, top)
    return jnp.take_along_axis(grid, (jnp.arange(top)[None, :] + turn) % top, axis=1)


def portions_of(number_of, total, bound, lean, full):
    loads = [(1 << 20) // math.isqrt(standing ** lean) + 1 for standing in range(1, number_of + 1)]
    largest = bound if full else min(bound, max(-(-total // number_of), total * loads[0] // sum(loads)))
    least = 1 if total - largest >= number_of - 1 else 0
    holding, rest = [largest] + [least] * (number_of - 1), total - largest - least * (number_of - 1)
    while rest > 0:
        movable = [i for i in range(1, number_of) if holding[i] < largest] or [i for i in range(1, number_of) if holding[i] < bound]
        pool, budget = sum([loads[i] for i in movable]), rest
        for i in movable:
            more = min(bound - holding[i], max(1, budget * loads[i] // pool), rest)
            holding[i] = holding[i] + more
            rest = rest - more
    return np.array(holding)


def bell_draw(rng, shape, scale, reach, pieces=(), kind=jnp.bfloat16):
    loudness = shard_levels(rng, shape, pieces, -0.22, 0.18) if pieces else 1.0
    drawn = jax.random.normal(rng, shape, jnp.float32) * scale * loudness
    return jnp.minimum(jnp.maximum(drawn, -reach), reach).astype(kind)


def setup_inputs(seed: int = 0) -> dict:
    streams_of = jax.random.split(jax.random.key(seed), 11)
    moe_in = bell_draw(streams_of[0], (TOKENS, D), 1.0, 6.0, ((0, 128),))
    route_expert_keys = jax.random.split(jax.random.fold_in(streams_of[1], 1), TOKENS // TOK_DEV)
    route_expert_turns = jax.random.permutation(jax.random.fold_in(streams_of[1], 3), TOKENS // TOK_DEV)
    route_expert = jax.vmap(lambda own, number: routed_block(jax.random.fold_in(streams_of[1], 2), own, number, TOK_DEV, EXPERTS, TOPK, CAP, 2))(route_expert_keys, route_expert_turns).reshape((TOKENS, TOPK))
    route_weight = jnp.clip(jnp.exp(math.log(1.0) - 2.9957323 * jax.random.uniform(streams_of[2], (TOKENS, TOPK), jnp.float32) ** shard_levels(streams_of[2], (TOKENS, TOPK), ((0, 128),), -0.2, 0.2)), 0.05, 1.0)
    expert_gate_up = bell_draw(streams_of[3], (2 * EXPERTS, D, FFE), D ** -0.5, 0.09375, ((0, 128),))
    expert_down = bell_draw(streams_of[4], (2 * EXPERTS, FFE // 2, D), FFE ** -0.5, 0.15625, ((0, 128),))
    kv_cache = draw_kv_cache(jax.random.fold_in(streams_of[10], 71), 0)
    decode_query = draw_decode_query(jax.random.fold_in(streams_of[10], 71), 0)
    new_kv = bell_draw(streams_of[7], (PROMPTS, 2 * KVH * HD), 1.0, 6.0, ((0, 128),))
    kv_length = uneven(streams_of[8], PROMPTS, PROMPTS * L // 2, L, 1).astype(jnp.int32)
    decode_group_keys = jax.random.split(jax.random.fold_in(streams_of[9], 1), PROMPTS // P_DEV)
    decode_group_turns = jax.random.permutation(jax.random.fold_in(streams_of[9], 3), PROMPTS // P_DEV)
    decode_group = jax.vmap(lambda own, number: routed_block(jax.random.fold_in(streams_of[9], 2), own, number, P_DEV, N_DP, 1, MOSTP, 2))(decode_group_keys, decode_group_turns).reshape((PROMPTS, 1))
    return dict(moe_in=moe_in, route_expert=route_expert, route_weight=route_weight, expert_gate_up=expert_gate_up, expert_down=expert_down, kv_cache=kv_cache, decode_query=decode_query, new_kv=new_kv, kv_length=kv_length, decode_group=decode_group)


def place_rows(owners, groups, capacity):
    flattened = owners.reshape(-1)
    onehot = (flattened[:, None] == jnp.arange(groups, dtype=jnp.int32)[None, :]).astype(jnp.int32)
    earlier = jnp.cumsum(onehot, axis=0) - onehot
    return flattened * capacity + lax.optimization_barrier(jnp.sum(earlier * onehot, axis=1))

def expert_half(rows, gate_up, down_proj):
    half_units = down_proj.shape[0]
    joint = jnp.dot(rows, gate_up, preferred_element_type=jnp.float32)
    hidden_units = (jax.nn.silu(joint[:, :half_units]) * joint[:, half_units:]).astype(jnp.bfloat16)
    return jnp.dot(hidden_units, down_proj, preferred_element_type=jnp.float32).astype(jnp.bfloat16)

def reference(moe_in, route_expert, route_weight, expert_gate_up, expert_down, kv_cache, decode_query, new_kv, kv_length, decode_group):
    route_share = route_weight / lax.optimization_barrier(jnp.sum(route_weight, axis=1, keepdims=True))
    flat_ids = route_expert.reshape(-1)
    flat_share = route_share.reshape(-1)
    limit = N_DP * N_EXPERT * CAP

    def one_expert(carry, expert_id):
        chosen = flat_ids == expert_id
        where_rows = jnp.nonzero(chosen, size=limit, fill_value=0)[0].astype(jnp.int32)
        valid = jnp.arange(limit, dtype=jnp.int32) < jnp.sum(chosen.astype(jnp.int32))
        token_ids = where_rows // TOPK
        rows = moe_in[token_ids]
        first = expert_half(rows, expert_gate_up[2 * expert_id], expert_down[2 * expert_id])
        second = expert_half(rows, expert_gate_up[2 * expert_id + 1], expert_down[2 * expert_id + 1])
        expert_sum = first.astype(jnp.float32) + second.astype(jnp.float32)
        term = jnp.where(valid[:, None], flat_share[where_rows][:, None] * expert_sum, 0.0)
        return (carry.at[token_ids].add(term), None)
    start = jnp.zeros((TOKENS, D), jnp.float32)
    total, _ = lax.scan(one_expert, start, jnp.arange(EXPERTS, dtype=jnp.int32))
    moe_out = total.astype(jnp.bfloat16)
    blocks_ids = decode_group.reshape(N_DP, P_DEV)
    seat = jax.vmap(lambda owners: place_rows(owners, N_DP, MOSTP))(blocks_ids)
    source_index = jnp.arange(N_DP, dtype=jnp.int32)[:, None]
    slot_row = seat // MOSTP * SLOTS + source_index * MOSTP + seat % MOSTP
    decode_cache = jnp.zeros((N_DP * SLOTS, L, 2 * KVH * HD), jnp.bfloat16).at[slot_row.reshape(-1)].set(kv_cache)
    groups_per = H // KVH
    blocks = L // BLK
    scale = 1.0 / math.sqrt(HD)
    keys = kv_cache[:, :, :KVH * HD].reshape(PROMPTS, blocks, BLK, KVH, HD)
    values = kv_cache[:, :, KVH * HD:].reshape(PROMPTS, blocks, BLK, KVH, HD)
    query = decode_query.reshape(PROMPTS, KVH, groups_per, HD)
    score = jnp.einsum('skgd,sbpkd->skgbp', query.astype(jnp.float32), keys.astype(jnp.float32)) * scale
    position = jnp.arange(L, dtype=jnp.int32).reshape(blocks, BLK)
    live = (position[None] < kv_length[:, None, None])[:, None, None]
    block_max = lax.optimization_barrier(jnp.max(jnp.where(live, score, -1e+30), axis=-1))
    block_weight = jnp.where(live, jnp.exp(score - block_max[..., None]), 0.0)
    block_sum = lax.optimization_barrier(jnp.sum(block_weight, axis=-1))
    rounded_weight = block_weight.astype(jnp.bfloat16)
    block_acc = jnp.einsum('skgbp,sbpkd->skgbd', rounded_weight.astype(jnp.float32), values.astype(jnp.float32))
    new_key = new_kv[:, :KVH * HD].reshape(PROMPTS, KVH, HD)
    new_value = new_kv[:, KVH * HD:].reshape(PROMPTS, KVH, 1, HD).astype(jnp.float32)
    new_score = jnp.einsum('skgd,skd->skg', query.astype(jnp.float32), new_key.astype(jnp.float32)) * scale
    top_score = jnp.maximum(lax.optimization_barrier(jnp.max(block_max, axis=-1)), new_score)
    factor = jnp.exp(block_max - top_score[..., None])
    own = jnp.exp(new_score - top_score)
    total_weight = lax.optimization_barrier(jnp.sum(block_sum * factor, axis=-1)) + own
    accum = lax.optimization_barrier(jnp.sum(block_acc * factor[..., None], axis=3)) + own[..., None] * new_value
    decode_out = (accum / total_weight[..., None]).reshape(PROMPTS, H * HD).astype(jnp.bfloat16)
    return (moe_out, decode_cache, decode_out)
```

```python
import functools
import math

import jax
import jax.numpy as jnp
from jax import lax
from jax.experimental import pallas as pl
from jax.experimental.pallas import tpu as pltpu
from jax.sharding import Mesh, PartitionSpec as P

H = 64
KVH = 4
HD = 128
MOSTP = 2
TOPK = 8
CAP = 2
LANES = 128
ROWS = 16
PIECE = 256
PIECE_ROWS = ROWS * PIECE // LANES

very_low = -1e30

EVERY = ("dp", "z", "core")
CHIPS = ("dp", "z")
GROUP = ("z", "core")


def after(value, earlier):
    value, _ = lax.optimization_barrier((value, earlier))
    return value


def earlier_equal(ids):
    count = ids.shape[0]
    order = jnp.arange(count, dtype=jnp.int32)
    same = (ids[:, None] == ids[None, :]) & (order[None, :] < order[:, None])
    return jnp.sum(same.astype(jnp.int32), axis=1)


def expert_half(rows, gate_up, down_proj):
    half_units = down_proj.shape[0]
    joint = jnp.dot(rows, gate_up, preferred_element_type=jnp.float32)
    hidden_units = (jax.nn.silu(joint[:, :half_units]) * joint[:, half_units:]).astype(jnp.bfloat16)
    return jnp.dot(hidden_units, down_proj, preferred_element_type=jnp.float32).astype(jnp.bfloat16)


def local_attention(kv_rows, queries, new_rows, lengths):
    prompts, positions, _ = kv_rows.shape
    groups_per = H // KVH
    scale = 1.0 / math.sqrt(HD)
    keys = kv_rows[:, :, : KVH * HD].reshape(prompts, positions, KVH, HD)
    values = kv_rows[:, :, KVH * HD :].reshape(prompts, positions, KVH, HD)
    query = queries.reshape(prompts, KVH, groups_per, HD)
    score = jnp.einsum("skgd,spkd->skgp", query, keys, preferred_element_type=jnp.float32) * scale
    position = jnp.arange(positions, dtype=jnp.int32)
    live = (position[None] < lengths[:, None])[:, None, None]
    new_key = new_rows[:, : KVH * HD].reshape(prompts, KVH, HD)
    new_value = new_rows[:, KVH * HD :].reshape(prompts, KVH, 1, HD).astype(jnp.float32)
    new_score = (
        jnp.einsum("skgd,skd->skg", query, new_key, preferred_element_type=jnp.float32) * scale
    )
    top_score = jnp.maximum(jnp.max(jnp.where(live, score, very_low), axis=-1), new_score)
    weight = jnp.where(live, jnp.exp(score - top_score[..., None]), 0.0)
    own = jnp.exp(new_score - top_score)
    total_weight = jnp.sum(weight, axis=-1) + own
    accum = jnp.einsum(
        "skgp,spkd->skgd", weight.astype(jnp.bfloat16), values, preferred_element_type=jnp.float32
    )
    accum = accum + own[..., None] * new_value
    return (accum / total_weight[..., None]).astype(jnp.bfloat16).reshape(prompts, H * HD)


def pack_kernel(route_ref, kv_ref, tokens_ref, note_ref, out_ref, token_of, used):
    step = pl.program_id(0)
    topk_log = TOPK.bit_length() - 1

    @pl.when(step == 0)
    def _():
        @pl.loop(0, used.shape[0])
        def _(e):
            used[e] = 0

        @pl.loop(0, route_ref.shape[0])
        def _(j):
            e = route_ref[j]
            r = used[e]
            used[e] = r + 1
            token_of[e * CAP + r] = j >> topk_log

    mine, span, width = kv_ref.shape
    cuts = width // PIECE
    here = out_ref.shape[0]
    for d in range(here):
        at, cut = d // cuts, d % cuts
        for p in range(mine):
            for tile in range(PIECE // LANES):
                row = (p * (PIECE // LANES) + tile) * ROWS
                column = cut * PIECE + tile * LANES
                out_ref[d, row : row + ROWS, :] = kv_ref[
                    p, at * ROWS : (at + 1) * ROWS, column : column + LANES
                ]
        first = mine * PIECE_ROWS
        token_rows = tokens_ref.shape[1]
        out_ref[d, first : first + token_rows, :] = tokens_ref[token_of[step * here + d]]
        out_ref[d, first + token_rows :, :] = note_ref[...]


def pack(route, kv_cache, tokens, note):
    mine, positions, width = kv_cache.shape
    slots = route.shape[0]
    steps = 8
    rows = mine * PIECE_ROWS + tokens.shape[1] + note.shape[0]
    return pl.pallas_call(
        pack_kernel,
        out_shape=jax.ShapeDtypeStruct((slots, rows, LANES), jnp.bfloat16),
        grid=(steps,),
        in_specs=[
            pl.BlockSpec(memory_space=pltpu.SMEM),
            pl.BlockSpec((mine, positions // steps, width), lambda b: (0, b, 0)),
            pl.BlockSpec(tokens.shape, lambda b: (0, 0, 0)),
            pl.BlockSpec(note.shape, lambda b: (0, 0)),
        ],
        out_specs=pl.BlockSpec((slots // steps, rows, LANES), lambda b: (b, 0, 0)),
        scratch_shapes=[pltpu.SMEM((slots,), jnp.int32), pltpu.SMEM((slots // CAP,), jnp.int32)],
        compiler_params=pltpu.CompilerParams(vmem_limit_bytes=32 << 20),
        name="pack",
    )(route, kv_cache, tokens, note)


def seats_kernel(n_dp, groups_ref, pieces_ref, out_ref, used):
    rows_out = out_ref.shape[0]
    each = groups_ref.shape[0] // n_dp
    chunk = 16

    @pl.loop(0, rows_out // chunk)
    def _(b):
        out_ref[pl.ds(b * chunk, chunk)] = jnp.zeros((chunk,) + out_ref.shape[1:], out_ref.dtype)

    @pl.loop(0, n_dp)
    def _(i):
        for g in range(n_dp):
            used[g] = 0
        for j in range(each):
            g = groups_ref[i * each + j]
            c = used[g]
            used[g] = c + 1
            row = (g * n_dp + i) * MOSTP + c
            per = pieces_ref.shape[1] // PIECE_ROWS
            start = j % per * PIECE_ROWS
            out_ref[row] = pieces_ref[i * (each // per) + j // per, start : start + PIECE_ROWS, :]


def seats(groups, payload, n_dp, mine):
    rows_out = n_dp * n_dp * MOSTP
    return pl.pallas_call(
        functools.partial(seats_kernel, n_dp),
        out_shape=jax.ShapeDtypeStruct((rows_out, PIECE_ROWS, LANES), jnp.bfloat16),
        grid=(1,),
        in_specs=[
            pl.BlockSpec(memory_space=pltpu.SMEM),
            pl.BlockSpec((payload.shape[0], mine * PIECE_ROWS, LANES), lambda b: (0, 0, 0)),
        ],
        out_specs=pl.BlockSpec((rows_out, PIECE_ROWS, LANES), lambda b: (0, 0, 0)),
        scratch_shapes=[pltpu.SMEM((n_dp,), jnp.int32)],
        compiler_params=pltpu.CompilerParams(vmem_limit_bytes=40 << 20),
        name="seats",
    )(groups, payload)


def assemble_kernel(pieces_ref, out_ref):
    width = out_ref.shape[2]
    cuts = width // PIECE
    for d in range(pieces_ref.shape[0]):
        at, cut = d // cuts, d % cuts
        for r in range(out_ref.shape[0]):
            for tile in range(PIECE // LANES):
                column = cut * PIECE + tile * LANES
                out_ref[r, at * ROWS : (at + 1) * ROWS, column : column + LANES] = pieces_ref[
                    d, r, tile * ROWS : (tile + 1) * ROWS, :
                ]


def assemble(pieces, positions, width):
    devices, rows = pieces.shape[:2]
    steps = 8
    return pl.pallas_call(
        assemble_kernel,
        out_shape=jax.ShapeDtypeStruct((rows, positions, width), jnp.bfloat16),
        grid=(steps,),
        in_specs=[
            pl.BlockSpec((devices // steps, rows, PIECE_ROWS, LANES), lambda b: (b, 0, 0, 0))
        ],
        out_specs=pl.BlockSpec((rows, positions // steps, width), lambda b: (0, b, 0)),
        compiler_params=pltpu.CompilerParams(vmem_limit_bytes=32 << 20),
        cost_estimate=pl.CostEstimate(
            flops=0, bytes_accessed=4 * rows * positions * width, transcendentals=0
        ),
        name="assemble",
    )(pieces)


def combine_kernel(target_ref, share_ref, rows_ref, out_ref):
    @pl.loop(0, out_ref.shape[0])
    def _(t):
        total = jnp.zeros(out_ref.shape[1:], jnp.float32)
        for k in range(TOPK):
            at = t * TOPK + k
            total += share_ref[at] * rows_ref[target_ref[at]].astype(jnp.float32)
        out_ref[t] = total.astype(out_ref.dtype)


def combine(target, share, rows, tok_rows):
    return pl.pallas_call(
        combine_kernel,
        out_shape=jax.ShapeDtypeStruct((tok_rows,) + rows.shape[1:], jnp.bfloat16),
        in_specs=[
            pl.BlockSpec(memory_space=pltpu.SMEM),
            pl.BlockSpec(memory_space=pltpu.SMEM),
            pl.BlockSpec(memory_space=pltpu.VMEM),
        ],
        out_specs=pl.BlockSpec(memory_space=pltpu.VMEM),
        compiler_params=pltpu.CompilerParams(vmem_limit_bytes=32 << 20),
        name="combine",
    )(target, share, rows)


def per_device(
    moe_in,
    route_expert,
    route_weight,
    expert_gate_up,
    expert_down,
    kv_cache,
    decode_query,
    new_kv,
    kv_length,
    decode_group,
):
    tok_rows, model = moe_in.shape
    n_dp = lax.axis_size("dp")
    n_group = lax.axis_size("z") * lax.axis_size("core")
    devices = n_dp * n_group
    mine, positions, kv_width = kv_cache.shape
    token_lines = model // LANES
    swap = [(0, 1), (1, 0)]

    flat = route_expert.reshape(-1)
    note = jnp.pad(
        decode_group.astype(jnp.bfloat16).reshape(1, mine), ((0, 7), (0, LANES - mine))
    )
    payload = pack(flat, kv_cache, moe_in.reshape(tok_rows, token_lines, LANES), note)
    arrived = lax.all_to_all(payload, EVERY, split_axis=0, concat_axis=0, tiled=True)

    first = mine * PIECE_ROWS
    groups = arrived[:, first + token_lines, :mine].astype(jnp.int32).reshape(-1)
    routed = seats(groups, arrived, n_dp, mine)
    settled = lax.all_to_all(routed, EVERY, split_axis=0, concat_axis=0, tiled=True)

    answer = local_attention(kv_cache, decode_query, new_kv, kv_length)

    own_rows = arrived[:, first : first + token_lines, :].reshape(devices, model)
    other_rows = lax.ppermute(own_rows, "core", swap)
    part = expert_half(
        jnp.concatenate([own_rows, other_rows], axis=0), expert_gate_up[0], expert_down[0]
    )
    other_part = lax.ppermute(part[devices:], "core", swap)
    expert_sum = (part[:devices].astype(jnp.float32) + other_part.astype(jnp.float32)).astype(
        jnp.bfloat16
    )
    returned = lax.all_to_all(
        after(expert_sum.reshape(devices, token_lines, LANES), settled),
        EVERY,
        split_axis=0,
        concat_axis=0,
        tiled=True,
    )

    regrouped = assemble(
        settled.reshape(devices, -1, PIECE_ROWS, LANES), positions, kv_width
    )

    e = lax.axis_index("z") * lax.axis_size("core") + lax.axis_index("core")
    wide = answer.shape[1] // n_group
    by_owner = answer.reshape(mine, n_group, wide)
    by_shift = [lax.dynamic_index_in_dim(by_owner, e, 1, keepdims=False)]
    for shift in range(1, n_group):
        piece = lax.dynamic_index_in_dim(by_owner, (e + shift) % n_group, 1, keepdims=False)
        by_shift.append(
            lax.ppermute(piece, GROUP, [(d, (d + shift) % n_group) for d in range(n_group)])
        )
    decode_out = jnp.take(
        jnp.stack(by_shift), (e - jnp.arange(n_group, dtype=jnp.int32)) % n_group, axis=0
    ).reshape(mine * n_group, wide)

    route_share = route_weight / jnp.sum(route_weight, axis=1, keepdims=True)
    target = flat * CAP + earlier_equal(flat)
    moe_out = combine(target, route_share.reshape(-1), returned, tok_rows).reshape(
        tok_rows, model
    )
    return (moe_out, regrouped, decode_out)


def solution(mesh):
    n_dp, n_group = mesh.devices.shape
    fine = Mesh(mesh.devices.reshape(n_dp, n_group // 2, 2), ("dp", "z", "core"))
    return jax.shard_map(
        per_device,
        mesh=fine,
        in_specs=(
            P(EVERY, None),
            P(EVERY, None),
            P(EVERY, None),
            P(EVERY, None, None),
            P(EVERY, None, None),
            P(EVERY, None, None),
            P(EVERY, None),
            P(EVERY, None),
            P(EVERY),
            P(EVERY, None),
        ),
        out_specs=(P(EVERY, None), P(EVERY, None, None), P("dp", GROUP)),
        check_vma=False,
    )
```

```python
import functools
import math

import jax
import jax.numpy as jnp
from jax import lax
from jax.experimental import pallas as pl
from jax.experimental.pallas import tpu as pltpu
from jax.sharding import Mesh, PartitionSpec as P

H = 64
KVH = 4
HD = 128
MOSTP = 2
TOPK = 8
CAP = 2
CHIPS = 4
LANES = 128
ROWS = 16
PIECE = 256
PIECE_ROWS = ROWS * PIECE // LANES

very_low = -1e30

EVERY = ("dp", "z", "core")
ROUND = ("z", "core", "dp")
GROUP = ("z", "core")


def after(value, earlier):
    value, _ = lax.optimization_barrier((value, earlier))
    return value


def earlier_equal(ids):
    count = ids.shape[0]
    order = jnp.arange(count, dtype=jnp.int32)
    same = (ids[:, None] == ids[None, :]) & (order[None, :] < order[:, None])
    return jnp.sum(same.astype(jnp.int32), axis=1)


def expert_half(rows, gate_up, down_proj):
    half_units = down_proj.shape[0]
    joint = jnp.dot(rows, gate_up, preferred_element_type=jnp.float32)
    hidden_units = (jax.nn.silu(joint[:, :half_units]) * joint[:, half_units:]).astype(jnp.bfloat16)
    return jnp.dot(hidden_units, down_proj, preferred_element_type=jnp.float32).astype(jnp.bfloat16)


def local_attention(kv_rows, queries, new_rows, lengths):
    prompts, positions, _ = kv_rows.shape
    groups_per = H // KVH
    scale = 1.0 / math.sqrt(HD)
    keys = kv_rows[:, :, : KVH * HD].reshape(prompts, positions, KVH, HD)
    values = kv_rows[:, :, KVH * HD :].reshape(prompts, positions, KVH, HD)
    query = queries.reshape(prompts, KVH, groups_per, HD)
    score = jnp.einsum("skgd,spkd->skgp", query, keys, preferred_element_type=jnp.float32) * scale
    position = jnp.arange(positions, dtype=jnp.int32)
    live = (position[None] < lengths[:, None])[:, None, None]
    new_key = new_rows[:, : KVH * HD].reshape(prompts, KVH, HD)
    new_value = new_rows[:, KVH * HD :].reshape(prompts, KVH, 1, HD).astype(jnp.float32)
    new_score = (
        jnp.einsum("skgd,skd->skg", query, new_key, preferred_element_type=jnp.float32) * scale
    )
    top_score = jnp.maximum(jnp.max(jnp.where(live, score, very_low), axis=-1), new_score)
    weight = jnp.where(live, jnp.exp(score - top_score[..., None]), 0.0)
    own = jnp.exp(new_score - top_score)
    total_weight = jnp.sum(weight, axis=-1) + own
    accum = jnp.einsum(
        "skgp,spkd->skgd", weight.astype(jnp.bfloat16), values, preferred_element_type=jnp.float32
    )
    accum = accum + own[..., None] * new_value
    return (accum / total_weight[..., None]).astype(jnp.bfloat16).reshape(prompts, H * HD)


def pack_kernel(
    n_dp, route_ref, group_ref, kv_hbm, tokens_ref, out_hbm,
    kv, out, lines, token_of, used, came, left,
):
    mine, positions, width = kv.shape
    parts = came.shape[0]
    span = positions // parts
    here = out.shape[0] // parts

    def fetch(b):
        rows = pl.ds(pl.multiple_of(b * span, span), span)
        return pltpu.make_async_copy(kv_hbm.at[:, rows], kv.at[:, rows], came.at[b])

    def store(b):
        rows = pl.ds(pl.multiple_of(b * here, here), here)
        return pltpu.make_async_copy(out.at[rows], out_hbm.at[rows], left.at[b])

    @pl.loop(0, parts)
    def _(b):
        fetch(b).start()

    for e in range(used.shape[0]):
        used[e] = 0

    @pl.loop(0, route_ref.shape[1])
    def _(t):
        for k in range(TOPK):
            e = route_ref[k, t]
            r = used[e]
            used[e] = r + 1
            token_of[seat_of(e, r, n_dp)] = t

    for j in range(lines.shape[1]):
        lines[:, j, :] = tokens_ref[:, j * LANES : (j + 1) * LANES].astype(jnp.float32)

    first = mine * PIECE_ROWS
    token_rows = lines.shape[1]
    note_rows = out.shape[1] - first - token_rows
    lane = lax.broadcasted_iota(jnp.int32, (note_rows, LANES), 1)
    note = jnp.zeros((note_rows, LANES), jnp.float32)
    for p in range(mine):
        note = jnp.where(lane == p, group_ref[p].astype(jnp.float32), note)
    note = note.astype(out.dtype)
    cuts = width // PIECE

    @pl.loop(0, parts)
    def _(b):
        fetch(b).wait()
        for d in range(here):
            at, cut = d // cuts, d % cuts
            place = b * here + d
            rows = pl.ds(pl.multiple_of(b * span + at * ROWS, ROWS), ROWS)
            for p in range(mine):
                for tile in range(PIECE // LANES):
                    row = (p * (PIECE // LANES) + tile) * ROWS
                    column = cut * PIECE + tile * LANES
                    out[place, row : row + ROWS, :] = kv[p, rows, column : column + LANES]
            out[place, first : first + token_rows, :] = lines[token_of[place]].astype(out.dtype)
            out[place, first + token_rows :, :] = note
        store(b).start()

    @pl.loop(0, parts)
    def _(b):
        store(b).wait()


def seat_of(expert, r, n_dp):
    return ((expert & (CHIPS - 1)) * CAP + r) * n_dp + (expert >> (CHIPS.bit_length() - 1))


def pack(route, group, kv_cache, tokens, n_dp):
    mine, positions, width = kv_cache.shape
    tok_rows, model = tokens.shape
    slots = route.size
    parts = 8
    rows = mine * PIECE_ROWS + model // LANES + 8
    return pl.pallas_call(
        functools.partial(pack_kernel, n_dp),
        out_shape=jax.ShapeDtypeStruct((slots, rows, LANES), jnp.bfloat16),
        in_specs=[
            pl.BlockSpec(memory_space=pltpu.SMEM),
            pl.BlockSpec(memory_space=pltpu.SMEM),
            pl.BlockSpec(memory_space=pltpu.HBM),
            pl.BlockSpec(memory_space=pltpu.VMEM),
        ],
        out_specs=pl.BlockSpec(memory_space=pltpu.HBM),
        scratch_shapes=[
            pltpu.VMEM(kv_cache.shape, jnp.bfloat16),
            pltpu.VMEM((slots, rows, LANES), jnp.bfloat16),
            pltpu.VMEM((tok_rows, model // LANES, LANES), jnp.float32),
            pltpu.SMEM((slots,), jnp.int32),
            pltpu.SMEM((slots // CAP,), jnp.int32),
            pltpu.SemaphoreType.DMA((parts,)),
            pltpu.SemaphoreType.DMA((parts,)),
        ],
        compiler_params=pltpu.CompilerParams(vmem_limit_bytes=60 << 20),
        name="pack",
    )(route, group, kv_cache, tokens)


def seats_kernel(n_dp, n_group, groups_ref, pieces_ref, out_hbm, out, used, left):
    per = pieces_ref.shape[1] // PIECE_ROWS
    span = out.shape[0] // n_group
    chunk = 16

    def store(b):
        rows = pl.ds(pl.multiple_of(b * span, span), span)
        return pltpu.make_async_copy(out.at[rows], out_hbm.at[rows], left.at[b])

    @pl.loop(0, n_group)
    def _(b):
        for at in range(0, span, chunk):
            out[pl.ds(b * span + at, chunk)] = jnp.zeros((chunk,) + out.shape[1:], out.dtype)
        for odd in range(2):
            i = 2 * b + odd
            for g in range(n_dp):
                used[g] = 0
            for e in range(n_group):
                source = e * n_dp + i
                for p in range(per):
                    g = groups_ref[source * per + p]
                    c = used[g]
                    used[g] = c + 1
                    row = b * span + (g * 2 + odd) * MOSTP + c
                    start = p * PIECE_ROWS
                    out[row] = pieces_ref[source, start : start + PIECE_ROWS, :]
        store(b).start()

    @pl.loop(0, n_group)
    def _(b):
        store(b).wait()


def seats(groups, payload, n_dp, n_group, mine):
    rows_out = n_dp * n_dp * MOSTP
    return pl.pallas_call(
        functools.partial(seats_kernel, n_dp, n_group),
        out_shape=jax.ShapeDtypeStruct((rows_out, PIECE_ROWS, LANES), jnp.bfloat16),
        grid=(1,),
        in_specs=[
            pl.BlockSpec(memory_space=pltpu.SMEM),
            pl.BlockSpec((payload.shape[0], mine * PIECE_ROWS, LANES), lambda b: (0, 0, 0)),
        ],
        out_specs=pl.BlockSpec(memory_space=pltpu.HBM),
        scratch_shapes=[
            pltpu.VMEM((rows_out, PIECE_ROWS, LANES), jnp.bfloat16),
            pltpu.SMEM((n_dp,), jnp.int32),
            pltpu.SemaphoreType.DMA((n_group,)),
        ],
        compiler_params=pltpu.CompilerParams(vmem_limit_bytes=50 << 20),
        name="seats",
    )(groups, payload)


def assemble_kernel(pieces_ref, out_ref):
    width = out_ref.shape[2]
    cuts = width // PIECE
    for d in range(pieces_ref.shape[0]):
        at, cut = d // cuts, d % cuts
        for r in range(out_ref.shape[0]):
            for tile in range(PIECE // LANES):
                column = cut * PIECE + tile * LANES
                out_ref[r, at * ROWS : (at + 1) * ROWS, column : column + LANES] = pieces_ref[
                    d, r, tile * ROWS : (tile + 1) * ROWS, :
                ]


def assemble(pieces, positions, width):
    devices, rows = pieces.shape[:2]
    steps = 8
    return pl.pallas_call(
        assemble_kernel,
        out_shape=jax.ShapeDtypeStruct((rows, positions, width), jnp.bfloat16),
        grid=(steps,),
        in_specs=[
            pl.BlockSpec((devices // steps, rows, PIECE_ROWS, LANES), lambda b: (b, 0, 0, 0))
        ],
        out_specs=pl.BlockSpec((rows, positions // steps, width), lambda b: (0, b, 0)),
        compiler_params=pltpu.CompilerParams(vmem_limit_bytes=32 << 20),
        cost_estimate=pl.CostEstimate(
            flops=0, bytes_accessed=4 * rows * positions * width, transcendentals=0
        ),
        name="assemble",
    )(pieces)


def combine_kernel(target_ref, share_ref, rows_ref, out_ref, lines):
    for t in range(out_ref.shape[0]):
        total = jnp.zeros(lines.shape[1:], jnp.float32)
        for k in range(TOPK):
            at = t * TOPK + k
            total += share_ref[at] * rows_ref[target_ref[at]].astype(jnp.float32)
        lines[t] = total
    for j in range(lines.shape[1]):
        out_ref[:, j * LANES : (j + 1) * LANES] = lines[:, j, :].astype(out_ref.dtype)


def combine(target, share, rows, tok_rows):
    token_lines = rows.shape[1]
    return pl.pallas_call(
        combine_kernel,
        out_shape=jax.ShapeDtypeStruct((tok_rows, token_lines * LANES), jnp.bfloat16),
        in_specs=[
            pl.BlockSpec(memory_space=pltpu.SMEM),
            pl.BlockSpec(memory_space=pltpu.SMEM),
            pl.BlockSpec(memory_space=pltpu.VMEM),
        ],
        out_specs=pl.BlockSpec(memory_space=pltpu.VMEM),
        scratch_shapes=[pltpu.VMEM((tok_rows, token_lines, LANES), jnp.float32)],
        compiler_params=pltpu.CompilerParams(vmem_limit_bytes=32 << 20),
        name="combine",
    )(target, share, rows)


def per_device(
    moe_in,
    route_expert,
    route_weight,
    expert_gate_up,
    expert_down,
    kv_cache,
    decode_query,
    new_kv,
    kv_length,
    decode_group,
):
    tok_rows, model = moe_in.shape
    n_dp = lax.axis_size("dp")
    n_group = lax.axis_size("z") * lax.axis_size("core")
    devices = n_dp * n_group
    mine, positions, kv_width = kv_cache.shape
    token_lines = model // LANES
    swap = [(0, 1), (1, 0)]

    payload = pack(route_expert.T, decode_group.reshape(-1), kv_cache, moe_in, n_dp)
    arrived = lax.all_to_all(payload, ROUND, split_axis=0, concat_axis=0, tiled=True)

    first = mine * PIECE_ROWS
    groups = arrived[:, first + token_lines, :mine].astype(jnp.int32).reshape(-1)
    routed = seats(groups, arrived, n_dp, n_group, mine)
    settled = lax.all_to_all(routed, ROUND, split_axis=0, concat_axis=0, tiled=True)

    answer = local_attention(kv_cache, decode_query, new_kv, kv_length)

    own_rows = arrived[:, first : first + token_lines, :].reshape(devices, model)
    other_rows = lax.ppermute(own_rows, "core", swap)
    part = expert_half(
        jnp.concatenate([own_rows, other_rows], axis=0), expert_gate_up[0], expert_down[0]
    )
    other_part = lax.ppermute(part[devices:], "core", swap)
    expert_sum = (part[:devices].astype(jnp.float32) + other_part.astype(jnp.float32)).astype(
        jnp.bfloat16
    )
    returned = lax.all_to_all(
        after(expert_sum.reshape(devices, token_lines, LANES), settled),
        ROUND,
        split_axis=0,
        concat_axis=0,
        tiled=True,
    )

    regrouped = assemble(
        settled.reshape(devices, -1, PIECE_ROWS, LANES), positions, kv_width
    )

    e = lax.axis_index("z") * lax.axis_size("core") + lax.axis_index("core")
    wide = answer.shape[1] // n_group
    by_owner = answer.reshape(mine, n_group, wide)
    by_shift = [lax.dynamic_index_in_dim(by_owner, e, 1, keepdims=False)]
    for shift in range(1, n_group):
        piece = lax.dynamic_index_in_dim(by_owner, (e + shift) % n_group, 1, keepdims=False)
        by_shift.append(
            lax.ppermute(piece, GROUP, [(d, (d + shift) % n_group) for d in range(n_group)])
        )
    decode_out = jnp.take(
        jnp.stack(by_shift), (e - jnp.arange(n_group, dtype=jnp.int32)) % n_group, axis=0
    ).reshape(mine * n_group, wide)

    route_share = route_weight / jnp.sum(route_weight, axis=1, keepdims=True)
    flat = route_expert.reshape(-1)
    target = seat_of(flat, earlier_equal(flat), n_dp)
    moe_out = combine(target, route_share.reshape(-1), returned, tok_rows)
    return (moe_out, regrouped, decode_out)


def solution(mesh):
    n_dp, n_group = mesh.devices.shape
    fine = Mesh(mesh.devices.reshape(n_dp, n_group // 2, 2), ("dp", "z", "core"))
    return jax.shard_map(
        per_device,
        mesh=fine,
        in_specs=(
            P(EVERY, None),
            P(EVERY, None),
            P(EVERY, None),
            P(EVERY, None, None),
            P(EVERY, None, None),
            P(EVERY, None, None),
            P(EVERY, None),
            P(EVERY, None),
            P(EVERY),
            P(EVERY, None),
        ),
        out_specs=(P(EVERY, None), P(EVERY, None, None), P("dp", GROUP)),
        check_vma=False,
    )
```
